32 devices in a mesh: groups: 2 (over y), pipe: 4 (over z), dp: 4 (over x, core).
Axes of the slice: x: 2, y: 2, z: 4, core: 2. Of those that a mesh axis runs over, the one named last changes fastest.
Arguments:
- section_input: bfloat16 [4, 32, 64, 768], P('pipe', ('groups', 'dp')), parts along dimension 1, may hold values from -6 to 6
- depth_kernel: bfloat16 [4, 49, 768], P('pipe'), may hold values from -0.875 to 0.875
- norm_gain: bfloat16 [4, 768], P('pipe'), may hold values from 0.5 to 1.5
- expand_weight: bfloat16 [4, 768, 3072], P('pipe', 'dp'), may hold values from -0.21875 to 0.21875
- shrink_weight: bfloat16 [4, 3072, 768], P('pipe', 'dp'), may hold values from -0.02734375 to 0.02734375
- response_gain: bfloat16 [4, 3072], P('pipe'), may hold values from -3 to 3
- loss_grad: bfloat16 [32, 64, 768], P(('groups', 'dp')), parts along dimension 0, may hold values from -6 to 6
- plan: int32 [8, 4], P(('groups', 'dp')), parts along dimension 0, may hold values from 0 to 3, each once within a row
Outputs:
- input_grad: bfloat16 [4, 32, 64, 768], P('pipe', ('groups', 'dp')), parts along dimension 1
- kernel_grad: float32 [8, 49, 768], P(('groups', 'pipe'), None, 'dp'), parts along dimension 0
- response_grad: float32 [8, 3072], P(('groups', 'pipe'), 'dp'), parts along dimension 0
The draws below stay inside these ranges and needn't reach their ends.
There are 2 independent parts, one for each index of `groups`. The reference program is written for one: setup_inputs(seed, part) draws one part's arguments, and reference() takes and returns one part's arrays. A program takes and returns all parts, laid end to end along the dimension named above; an argument that names none is the same for every part. Nothing has to cross between parts.
Inputs may be any that keep to these rules, and one draw needn't show every extreme that they name: `plan`: each row holds each of the 4 micro-batch numbers once.
All inputs are finite; a program needn't handle non-finite values.
Results may differ from the reference program's by a relative error of at most 0.011.
Values may be sent and summed in bfloat16 or wider, within the bound.
A program may use at most 128 MiB of HBM per device.

```python
import jax
import jax.numpy as jnp
from jax import lax

C = 768
F = 3072
KSIDE = 7
SIDE = 8
MICRO = 4
TAPS = 49
PIX = 64
SECTIONS = 4
BATCH = 16
N_DP = 4


def steps_of(key, shape, cuts, least, top_value):
    loudness = 1.0
    for axis_at, blocks in cuts:
        draws = jax.random.uniform(jax.random.fold_in(jax.random.fold_in(key, 6), axis_at), (blocks,), jnp.float32, least / len(cuts), top_value / len(cuts))
        loudness = loudness * jnp.repeat(jnp.exp(draws), shape[axis_at] // blocks).reshape((-1,) + (1,) * (len(shape) - 1 - axis_at))
    return loudness


def noise(rng, extent, scale, limit, cuts=(), held_as=jnp.bfloat16):
    result = jax.random.normal(rng, extent, jnp.float32) * scale
    if len(cuts) > 0:
        result = steps_of(rng, extent, cuts, -0.22, 0.18) * result
    return jnp.clip(result, min=-limit, max=limit).astype(held_as)


def setup_inputs(seed: int = 0, part: int = 0) -> dict:
    key_list = jax.random.split(jax.random.key(seed), 9)
    part_keys = jax.random.split(jax.random.fold_in(key_list[8], part), 9)
    section_input = noise(part_keys[0], (SECTIONS, BATCH, PIX, C), 1.0, 6.0, ((0, 4), (1, 4)))
    depth_kernel = noise(key_list[1], (SECTIONS, TAPS, C), TAPS ** -0.5, 0.875, ((0, 4),))
    norm_gain = jnp.clip(0.5 + 1.0 * jax.random.uniform(key_list[2], (SECTIONS, C), jnp.float32) ** steps_of(key_list[2], (SECTIONS, C), ((0, 4),), -0.2, 0.2), 0.5, 1.5).astype(jnp.bfloat16)
    expand_weight = noise(key_list[3], (SECTIONS, C, F), C ** -0.5, 0.21875, ((0, 4), (1, 4)))
    shrink_weight = noise(key_list[4], (SECTIONS, F, C), (16 * F) ** -0.5, 0.02734375, ((0, 4), (1, 4)))
    response_gain = noise(key_list[5], (SECTIONS, F), 0.5, 3.0, ((0, 4),))
    loss_grad = noise(part_keys[6], (BATCH, PIX, C), 1.0, 6.0, ((0, 4),))
    plan = jax.vmap(lambda own: jax.random.permutation(own, MICRO))(jax.random.split(part_keys[7], N_DP)).reshape((N_DP, MICRO)).astype(jnp.int32)
    return {"section_input": section_input, "depth_kernel": depth_kernel, "norm_gain": norm_gain, "expand_weight": expand_weight, "shrink_weight": shrink_weight, "response_gain": response_gain, "loss_grad": loss_grad, "plan": plan}


inverse_root_two = 0.7071067811865476
inverse_root_tau = 0.3989422804014327

def depth_forward(images, kernel):
    margin = KSIDE // 2
    padded = jnp.pad(images, ((0, 0), (margin, margin), (margin, margin), (0, 0)))
    total = jnp.zeros_like(images)
    for row_tap in range(KSIDE):
        for col_tap in range(KSIDE):
            total = total + kernel[row_tap * KSIDE + col_tap] * padded[:, row_tap:row_tap + SIDE, col_tap:col_tap + SIDE, :]
    return total

def depth_transpose(gradient, kernel):
    margin = KSIDE // 2
    padded = jnp.pad(gradient, ((0, 0), (margin, margin), (margin, margin), (0, 0)))
    total = jnp.zeros_like(gradient)
    for row_tap in range(KSIDE):
        for col_tap in range(KSIDE):
            row_at = KSIDE - 1 - row_tap
            col_at = KSIDE - 1 - col_tap
            total = total + kernel[row_tap * KSIDE + col_tap] * padded[:, row_at:row_at + SIDE, col_at:col_at + SIDE, :]
    return total

def depth_kernel_terms(gradient, images):
    margin = KSIDE // 2
    padded = jnp.pad(images, ((0, 0), (margin, margin), (margin, margin), (0, 0)))
    pieces = []
    for row_tap in range(KSIDE):
        for col_tap in range(KSIDE):
            pieces.append(lax.optimization_barrier(jnp.sum(gradient * padded[:, row_tap:row_tap + SIDE, col_tap:col_tap + SIDE, :], axis=(0, 1, 2))))
    return jnp.stack(pieces)

def block_forward(grid_view, kernel, gain_vec, expand):
    channels = grid_view.shape[-1]
    images = grid_view.astype(jnp.float32)
    mixed = depth_forward(images, kernel)
    flattened = mixed.reshape(-1, channels)
    centre = lax.optimization_barrier(jnp.mean(flattened, axis=-1, keepdims=True))
    offset = flattened - centre
    spread = lax.rsqrt(lax.optimization_barrier(jnp.mean(offset * offset, axis=-1, keepdims=True)) + 1e-06)
    normed = offset * spread
    scaled = (normed * gain_vec).astype(jnp.bfloat16)
    hidden = jnp.dot(scaled, expand, preferred_element_type=jnp.float32)
    return (normed, spread, hidden)

def block_backward(upstream, grid_view, normed, spread, hidden, kernel, gain_vec, resp_gain, expand, shrink):
    image_count = grid_view.shape[0]
    channels = grid_view.shape[-1]
    units = hidden.shape[-1]
    images = grid_view.astype(jnp.float32)
    back_resp = lax.dot_general(upstream, shrink, (((1,), (1,)), ((), ())), preferred_element_type=jnp.float32)
    erf_part = 0.5 * (1.0 + lax.erf(hidden * inverse_root_two))
    activation = (hidden * erf_part).reshape(image_count, -1, units)
    back_image = back_resp.reshape(image_count, -1, units)
    energy = jnp.sqrt(lax.optimization_barrier(jnp.sum(activation * activation, axis=1, keepdims=True)) + 1e-06)
    average = lax.optimization_barrier(jnp.mean(energy, axis=2, keepdims=True)) + 1e-06
    norm_ratio = energy / average
    weighted = lax.optimization_barrier(jnp.sum(back_image * activation, axis=1, keepdims=True)) * resp_gain
    back_energy = weighted / average - lax.optimization_barrier(jnp.sum(weighted * energy, axis=2, keepdims=True)) / (average * average * units)
    back_activ = back_image * (1.0 + resp_gain * norm_ratio) + activation * (back_energy / energy)
    gelu_slope = erf_part + hidden * jnp.exp(-0.5 * hidden * hidden) * inverse_root_tau
    back_hidden = (back_activ.reshape(-1, units) * gelu_slope).astype(jnp.bfloat16)
    back_scaled = lax.dot_general(back_hidden, expand, (((1,), (1,)), ((), ())), preferred_element_type=jnp.float32)
    scaled_grad = back_scaled * gain_vec
    back_mixed = (scaled_grad - lax.optimization_barrier(jnp.mean(scaled_grad, axis=-1, keepdims=True)) - normed * lax.optimization_barrier(jnp.mean(scaled_grad * normed, axis=-1, keepdims=True))) * spread
    back_grid = back_mixed.reshape(image_count, SIDE, SIDE, channels)
    branch = depth_transpose(back_grid, kernel).reshape(-1, channels)
    grad_in = (upstream.astype(jnp.float32) + branch).astype(jnp.bfloat16)
    kernel_term = depth_kernel_terms(back_grid, images)
    gain_term = lax.optimization_barrier(jnp.sum(back_image * activation * norm_ratio, axis=(0, 1)))
    return (grad_in, kernel_term, gain_term)

def reference(section_input, depth_kernel, norm_gain, expand_weight, shrink_weight, response_gain, loss_grad, plan):
    channels = section_input.shape[-1]
    picker = (plan[:, :, None] == jnp.arange(MICRO, dtype=jnp.int32)[None, None, :]).astype(jnp.float32)
    slots = loss_grad.astype(jnp.float32).reshape(N_DP, MICRO, -1, channels)
    arranged = jnp.einsum('djm,djpc->dmpc', picker, slots).astype(jnp.bfloat16).reshape(loss_grad.shape)

    def section(state_now, params):
        section_x, kernel_raw, gain_raw, expand, shrink, resp_raw = params
        kernel = kernel_raw.astype(jnp.float32)
        gain_vec = gain_raw.astype(jnp.float32)
        resp_gain = resp_raw.astype(jnp.float32)
        grid_view = section_x.reshape(-1, SIDE, SIDE, channels)
        normed, spread, hidden = block_forward(grid_view, kernel, gain_vec, expand)
        grad_in, kernel_term, gain_term = block_backward(state_now.reshape(-1, channels), grid_view, normed, spread, hidden, kernel, gain_vec, resp_gain, expand, shrink)
        grad_in = grad_in.reshape(state_now.shape)
        return (grad_in, (grad_in, kernel_term, gain_term))
    leftover, outputs = lax.scan(section, arranged, (section_input, depth_kernel, norm_gain, expand_weight, shrink_weight, response_gain), reverse=True)
    return (outputs[0], outputs[1], outputs[2])
```

```python
import functools

import jax
import jax.numpy as jnp
from jax import lax
from jax.experimental import pallas as pl
from jax.experimental.pallas import tpu as pltpu
from jax.sharding import PartitionSpec as P

KSIDE = 7
SIDE = 8
MARGIN = 3
TAPS = KSIDE * KSIDE
LANES = 128
WINDOW = 256

inverse_root_two = 0.7071067811865476
inverse_root_tau = 0.3989422804014327

MESH = pl.DeviceIdType.MESH
CHUNKS = 3
F_BLOCK = 512
NT = (((1,), (1,)), ((), ()))


def shifted(value, by):
    if by == 0:
        return value
    column = lax.broadcasted_iota(jnp.int32, value.shape, 1) + by
    moved = pltpu.roll(value, (-by) % SIDE, 1)
    return jnp.where((column >= 0) & (column < SIDE), moved, 0.0)


def row_padded(value):
    zeros = jnp.zeros((MARGIN,) + value.shape[1:], value.dtype)
    return jnp.concatenate([zeros, value, zeros], axis=0)


def kernel(
    sections,
    x_ref,
    tap_ref,
    gain_ref,
    expand_ref,
    shrink_ref,
    resp_ref,
    loss_ref,
    grad_ref,
    share_ref,
    ew,
    sw,
    taps,
    mixed,
    normed,
    spread,
    scaled,
    hid,
    act,
    energy,
    ratio,
    sums,
    back,
    back_hid,
    side_steps,
    tap_acc,
    resp_acc,
    inbox,
    stage,
    landed,
    local_sem,
    x_send,
    x_recv,
    y_send,
    y_recv,
    own_send,
    own_recv,
    f_send,
    f_recv,
    h_send,
    h_recv,
    p_send,
    p_recv,
    s_send,
    s_recv,
):
    micro, pix, channels = x_ref.shape
    units = sw.shape[0]
    e_rows, s_rows = expand_ref.shape[0], shrink_ref.shape[0]
    grp = lax.axis_index("groups")
    pos = lax.axis_index("pipe")
    me = lax.axis_index("dp")
    last = sections - 1
    high, low = me // 2, me % 2
    across = 2 * (1 - high) + low
    beside = 2 * high + (1 - low)
    other = 2 * (1 - high) + (1 - low)

    barrier = pltpu.get_barrier_semaphore()

    def greet(g, p, d):
        pl.semaphore_signal(barrier, inc=1, device_id=(g, p, d), device_id_type=MESH)

    greet(grp, pos, across)
    greet(grp, pos, beside)
    greet(grp, pos, other)
    greet(1 - grp, pos, me)

    @pl.when(pos > 0)
    def _():
        greet(grp, pos - 1, me)

    @pl.when(pos < last)
    def _():
        greet(grp, pos + 1, me)

    pl.semaphore_wait(
        barrier, 4 + jnp.where(pos > 0, 1, 0) + jnp.where(pos < last, 1, 0)
    )

    def piece(owner, half, c):
        if c < CHUNKS:
            size = e_rows // (2 * CHUNKS)
            start = owner * e_rows + half * (e_rows // 2) + c * size
            return ew.at[pl.ds(pl.multiple_of(start, 16), size), :]
        size = s_rows // (2 * CHUNKS)
        start = owner * s_rows + half * (s_rows // 2) + (c - CHUNKS) * size
        return sw.at[pl.ds(pl.multiple_of(start, 16), size), :]

    def own_piece(half, c):
        if c < CHUNKS:
            size = e_rows // (2 * CHUNKS)
            start = half * (e_rows // 2) + c * size
            return expand_ref.at[pl.ds(pl.multiple_of(start, 16), size), :]
        size = s_rows // (2 * CHUNKS)
        start = half * (s_rows // 2) + (c - CHUNKS) * size
        return shrink_ref.at[pl.ds(pl.multiple_of(start, 16), size), :]

    def remote(src, dst, send, recv, g, p, d):
        return pltpu.make_async_remote_copy(
            src_ref=src,
            dst_ref=dst,
            send_sem=send,
            recv_sem=recv,
            device_id=(g, p, d),
            device_id_type=MESH,
        )

    def x_copy(c, owner):
        return remote(
            own_piece(grp, c), piece(owner, grp, c), x_send.at[c], x_recv.at[c], grp, pos, across
        )

    def y_copy(c, half):
        spot = piece(across, half, c)
        return remote(spot, spot, y_send.at[c], y_recv.at[c], 1 - grp, pos, me)

    def f_copy(c, owner):
        spot = piece(owner, grp, c)
        return remote(spot, spot, f_send.at[c], f_recv.at[c], grp, pos, beside)

    def h_copy(c, owner):
        spot = piece(owner, 1 - grp, c)
        return remote(spot, spot, h_send.at[c], h_recv.at[c], grp, pos, beside)

    def shard(which, owner):
        if which == 0:
            return ew.at[pl.ds(pl.multiple_of(owner * e_rows, 16), e_rows), :]
        return sw.at[pl.ds(pl.multiple_of(owner * s_rows, 16), s_rows), :]

    def own_copy(which, owner):
        src = (expand_ref, shrink_ref)[which]
        return remote(
            src, shard(which, owner), own_send.at[which], own_recv.at[which], grp, pos, beside
        )

    for c in range(2 * CHUNKS):
        x_copy(c, me).start()
    for which in range(2):
        own_copy(which, me).start()
    locals_ = [
        pltpu.make_async_copy((expand_ref, shrink_ref)[w], shard(w, me), local_sem.at[w])
        for w in range(2)
    ]
    for copy in locals_:
        copy.start()

    def pass_x(c):
        x_copy(c, across).wait_recv()
        y_copy(c, grp).start()
        f_copy(c, across).start()

    def pass_y(c):
        y_copy(c, 1 - grp).wait_recv()
        h_copy(c, across).start()

    taps[...] = tap_ref[...].astype(jnp.float32)
    gain = gain_ref[...].astype(jnp.float32)

    def forward(slot):
        def tile(t, carry):
            lanes = pl.ds(pl.multiple_of(t * LANES, LANES), LANES)
            image = x_ref[slot, :, lanes].astype(jnp.float32).reshape(SIDE, SIDE, LANES)
            total = jnp.zeros_like(image)
            for col in range(KSIDE):
                moved = row_padded(shifted(image, col - MARGIN))
                for row in range(KSIDE):
                    tap = row * KSIDE + col
                    total = total + taps[tap : tap + 1, lanes][None] * moved[row : row + SIDE]
            mixed[:, lanes] = total.reshape(pix, LANES)
            return carry

        lax.fori_loop(0, channels // LANES, tile, 0)
        value = mixed[...]
        offset = value - jnp.mean(value, axis=-1, keepdims=True)
        scale = lax.rsqrt(jnp.mean(offset * offset, axis=-1, keepdims=True) + 1e-06)
        unit = offset * scale
        normed[slot] = unit
        spread[slot] = scale
        scaled[pl.ds(pl.multiple_of(slot * pix, pix), pix), :] = (unit * gain).astype(jnp.bfloat16)

    def forward_step(slot, carry):
        forward(slot)
        return carry

    lax.fori_loop(0, micro, forward_step, 0)
    tap_acc[...] = jnp.zeros_like(tap_acc)
    resp_acc[...] = jnp.zeros_like(resp_acc)

    pass_x(0)
    for c in range(1, CHUNKS + 1):
        pass_x(c)
        pass_y(c - 1)
    locals_[0].wait()
    own_copy(0, beside).wait_recv()
    for c in range(CHUNKS):
        f_copy(c, other).wait_recv()
        h_copy(c, other).wait_recv()

    def hidden_block(b, carry):
        cols = pl.ds(pl.multiple_of(b * F_BLOCK, F_BLOCK), F_BLOCK)
        result = jnp.dot(scaled[...], ew[:, cols], preferred_element_type=jnp.float32)
        hid[:, :, cols] = result.reshape(micro, pix, F_BLOCK)
        return carry

    lax.fori_loop(0, units // F_BLOCK, hidden_block, 0)

    resp_block = F_BLOCK

    def gelu(slot):
        def block(b, carry):
            cols = pl.ds(pl.multiple_of(b * resp_block, resp_block), resp_block)
            h = hid[slot, :, cols]
            erf_part = 0.5 * (1.0 + lax.erf(h * inverse_root_two))
            a = h * erf_part
            act[slot, :, cols] = a
            hid[slot, :, cols] = erf_part + h * jnp.exp(-0.5 * h * h) * inverse_root_tau
            energy[slot, :, cols] = jnp.sqrt(jnp.sum(a * a, axis=0, keepdims=True) + 1e-06)
            return carry

        lax.fori_loop(0, units // resp_block, block, 0)
        e = energy[slot]
        ratio[slot] = e / (jnp.mean(e, axis=-1, keepdims=True) + 1e-06)

    pending = [c for c in range(CHUNKS + 1, 2 * CHUNKS)]
    for slot in range(micro):
        gelu(slot)
        if pending:
            c = pending.pop(0)
            pass_x(c)
            pass_y(c - 1)
    for c in pending:
        pass_x(c)
        pass_y(c - 1)
    pass_y(2 * CHUNKS - 1)
    locals_[1].wait()
    own_copy(1, beside).wait_recv()
    for c in range(CHUNKS, 2 * CHUNKS):
        f_copy(c, other).wait_recv()
        h_copy(c, other).wait_recv()

    def give(slot):
        return remote(
            grad_ref.at[slot], inbox.at[slot], p_send.at[slot], p_recv.at[slot], grp, pos - 1, me
        )

    def take(slot):
        return remote(
            grad_ref.at[slot], inbox.at[slot], p_send.at[slot], p_recv.at[slot], grp, pos + 1, me
        )

    def backward(slot, carry):
        @pl.when(pos == last)
        def _():
            inbox[slot] = loss_ref[slot]

        @pl.when(pos < last)
        def _():
            take(slot).wait_recv()

        up = inbox[slot]
        average = jnp.mean(energy[slot], axis=-1, keepdims=True) + 1e-06
        weight = jnp.zeros((1, 1), jnp.float32)
        for b in range(units // F_BLOCK):
            cols = slice(b * F_BLOCK, (b + 1) * F_BLOCK)
            br = lax.dot_general(up, sw[cols, :], NT, preferred_element_type=jnp.float32)
            back[:, cols] = br
            s = jnp.sum(br * act[slot, :, cols], axis=0, keepdims=True)
            resp_acc[:, cols] += s * ratio[slot, :, cols]
            w = s * resp_ref[:, cols].astype(jnp.float32)
            sums[:, cols] = w
            weight += jnp.sum(w * energy[slot, :, cols], axis=-1, keepdims=True)
        weight = weight / (average * average * units)
        inverse = 1.0 / average
        for b in range(units // F_BLOCK):
            cols = slice(b * F_BLOCK, (b + 1) * F_BLOCK)
            first = 1.0 + resp_ref[:, cols].astype(jnp.float32) * ratio[slot, :, cols]
            second = (sums[:, cols] * inverse - weight) / energy[slot, :, cols]
            ba = back[:, cols] * first + act[slot, :, cols] * second
            back_hid[:, cols] = (ba * hid[slot, :, cols]).astype(jnp.bfloat16)
        bs = jnp.zeros((pix, channels), jnp.float32)
        for b in range(units // F_BLOCK):
            cols = slice(b * F_BLOCK, (b + 1) * F_BLOCK)
            bs += lax.dot_general(
                back_hid[:, cols], ew[:, cols], NT, preferred_element_type=jnp.float32
            )
        q = bs * gain
        unit = normed[slot]
        mixed[...] = (
            q
            - jnp.mean(q, axis=-1, keepdims=True)
            - unit * jnp.mean(q * unit, axis=-1, keepdims=True)
        ) * spread[slot]

        def tile(t, inner):
            lanes = pl.ds(pl.multiple_of(t * LANES, LANES), LANES)
            image = mixed[:, lanes].reshape(SIDE, SIDE, LANES)
            total = inbox[slot, :, lanes].astype(jnp.float32).reshape(SIDE, SIDE, LANES)
            for col in range(KSIDE):
                plain = shifted(image, MARGIN - col)
                side_steps[col, :, lanes] = plain.reshape(pix, LANES)
                moved = row_padded(plain)
                for row in range(KSIDE):
                    tap = row * KSIDE + col
                    at = KSIDE - 1 - row
                    total = total + taps[tap : tap + 1, lanes][None] * moved[at : at + SIDE]
            grad_ref[slot, :, lanes] = total.reshape(pix, LANES).astype(jnp.bfloat16)
            return inner

        lax.fori_loop(0, channels // LANES, tile, 0)

        @pl.when(pos > 0)
        def _():
            give(slot).start()

        def tap_tile(t, inner):
            lanes = pl.ds(pl.multiple_of(t * LANES, LANES), LANES)
            image = x_ref[slot, :, lanes].astype(jnp.float32).reshape(SIDE, SIDE, LANES)
            for col in range(KSIDE):
                moved = row_padded(side_steps[col, :, lanes].reshape(SIDE, SIDE, LANES))
                for row in range(KSIDE):
                    tap = row * KSIDE + col
                    at = KSIDE - 1 - row
                    tap_acc[tap, :, lanes] += jnp.sum(moved[at : at + SIDE] * image, axis=0)
            return inner

        lax.fori_loop(0, channels // LANES, tap_tile, 0)
        return carry

    lax.fori_loop(0, micro, backward, 0)

    totals = jnp.sum(tap_acc[...], axis=1)
    share = channels // 4
    pad = stage.shape[1] - TAPS - units // 4 // WINDOW
    for d in range(4):
        start = d * share // LANES * LANES
        rows = [totals[:, start : start + WINDOW]]
        for k in range(units // 4 // WINDOW):
            at = d * (units // 4) + k * WINDOW
            rows.append(resp_acc[:, at : at + WINDOW])
        rows.append(jnp.zeros((pad, WINDOW), jnp.float32))
        stage[d] = jnp.concatenate(rows, axis=0).astype(jnp.bfloat16)

    peers = (across, beside, other)

    def s_copy(k):
        return remote(stage.at[peers[k]], landed.at[k], s_send.at[k], s_recv.at[k], grp, pos, peers[k])

    for k in range(3):
        s_copy(k).start()
    total = stage[me].astype(jnp.float32)
    for k in range(3):
        s_copy(k).wait_recv()
        total = total + landed[k].astype(jnp.float32)
    share_ref[...] = total

    for k in range(3):
        s_copy(k).wait_send()
    for c in range(2 * CHUNKS):
        x_copy(c, me).wait_send()
        y_copy(c, grp).wait_send()
        f_copy(c, across).wait_send()
        h_copy(c, across).wait_send()
    for which in range(2):
        own_copy(which, me).wait_send()

    @pl.when(pos > 0)
    def _():
        def drain(slot, carry):
            give(slot).wait_send()
            return carry

        lax.fori_loop(0, micro, drain, 0)


def on_device(
    section_input,
    depth_kernel,
    norm_gain,
    expand_weight,
    shrink_weight,
    response_gain,
    loss_grad,
    plan,
):
    local_x = section_input[0]
    micro, pix, channels = local_x.shape
    units = expand_weight.shape[2]
    sections = lax.axis_size("pipe")
    me = lax.axis_index("dp")
    order = plan[0]

    def pick(value, index):
        return lax.dynamic_index_in_dim(value, index, 0, keepdims=False)

    arranged = jnp.stack([pick(local_x, order[j]) for j in range(micro)])
    f32, bf16 = jnp.float32, jnp.bfloat16
    vmem = pl.BlockSpec(memory_space=pltpu.VMEM)
    anywhere = pl.BlockSpec(memory_space=pl.ANY)
    dma = pltpu.SemaphoreType.DMA
    grads, shares = pl.pallas_call(
        functools.partial(kernel, sections),
        out_shape=(
            jax.ShapeDtypeStruct((micro, pix, channels), bf16),
            jax.ShapeDtypeStruct((64, WINDOW), f32),
        ),
        in_specs=[vmem, vmem, vmem, anywhere, anywhere, vmem, vmem],
        out_specs=(vmem, vmem),
        scratch_shapes=[
            pltpu.VMEM((channels, units), bf16),
            pltpu.VMEM((units, channels), bf16),
            pltpu.VMEM((TAPS, channels), f32),
            pltpu.VMEM((pix, channels), f32),
            pltpu.VMEM((micro, pix, channels), f32),
            pltpu.VMEM((micro, pix, 1), f32),
            pltpu.VMEM((micro * pix, channels), bf16),
            pltpu.VMEM((micro, pix, units), f32),
            pltpu.VMEM((micro, pix, units), f32),
            pltpu.VMEM((micro, 1, units), f32),
            pltpu.VMEM((micro, 1, units), f32),
            pltpu.VMEM((1, units), f32),
            pltpu.VMEM((pix, units), f32),
            pltpu.VMEM((pix, units), bf16),
            pltpu.VMEM((KSIDE, pix, channels), f32),
            pltpu.VMEM((TAPS, SIDE, channels), f32),
            pltpu.VMEM((1, units), f32),
            pltpu.VMEM((micro, pix, channels), bf16),
            pltpu.VMEM((4, 64, WINDOW), bf16),
            pltpu.VMEM((3, 64, WINDOW), bf16),
            dma((2,)),
            dma((2 * CHUNKS,)),
            dma((2 * CHUNKS,)),
            dma((2 * CHUNKS,)),
            dma((2 * CHUNKS,)),
            dma((2,)),
            dma((2,)),
            dma((2 * CHUNKS,)),
            dma((2 * CHUNKS,)),
            dma((2 * CHUNKS,)),
            dma((2 * CHUNKS,)),
            dma((micro,)),
            dma((micro,)),
            dma((3,)),
            dma((3,)),
        ],
        compiler_params=pltpu.CompilerParams(
            collective_id=0, has_side_effects=True, vmem_limit_bytes=52 * 1024 * 1024
        ),
    )(
        arranged,
        depth_kernel[0],
        norm_gain,
        expand_weight[0],
        shrink_weight[0],
        response_gain,
        loss_grad,
    )
    slots = jnp.arange(micro, dtype=jnp.int32)
    result = jnp.stack(
        [pick(grads, jnp.sum(jnp.where(order == m, slots, 0))) for m in range(micro)]
    )
    share = channels // 4
    start = me * share - me * share // LANES * LANES
    kern_share = lax.dynamic_slice(shares, (0, start), (TAPS, share))
    gain_share = shares[TAPS : TAPS + units // 4 // WINDOW].reshape(1, units // 4)
    return (result[None], kern_share[None], gain_share)


def solution(mesh):
    if mesh.shape["dp"] != 4 or mesh.shape["groups"] != 2:
        raise ValueError("unsupported mesh")
    placed = (
        P("pipe", ("groups", "dp"), None, None),
        P("pipe", None, None),
        P("pipe", None),
        P("pipe", "dp", None),
        P("pipe", "dp", None),
        P("pipe", None),
        P(("groups", "dp"), None, None),
        P(("groups", "dp"), None),
    )
    return jax.shard_map(
        on_device,
        mesh=mesh,
        in_specs=placed,
        out_specs=(
            P("pipe", ("groups", "dp"), None, None),
            P(("groups", "pipe"), None, "dp"),
            P(("groups", "pipe"), "dp"),
        ),
        check_vma=False,
    )
```

```python
import functools

import jax
import jax.numpy as jnp
from jax import lax
from jax.experimental import pallas as pl
from jax.experimental.pallas import tpu as pltpu
from jax.sharding import PartitionSpec as P

KSIDE = 7
SIDE = 8
MARGIN = 3
TAPS = KSIDE * KSIDE
LANES = 128
WINDOW = 256
PIECES = 3

inverse_root_two = 0.7071067811865476
inverse_root_tau = 0.3989422804014327

MESH = pl.DeviceIdType.MESH
CHUNKS = 6
F_BLOCK = 512
NT = (((1,), (1,)), ((), ()))


def shifted(value, by):
    if by == 0:
        return value
    column = lax.broadcasted_iota(jnp.int32, value.shape, 1) + by
    moved = pltpu.roll(value, (-by) % SIDE, 1)
    return jnp.where((column >= 0) & (column < SIDE), moved, 0.0)


def row_padded(value):
    zeros = jnp.zeros((MARGIN,) + value.shape[1:], value.dtype)
    return jnp.concatenate([zeros, value, zeros], axis=0)


def kernel(
    sections,
    plan_ref,
    x_ref,
    tap_ref,
    gain_ref,
    expand_ref,
    shrink_ref,
    resp_ref,
    loss_ref,
    out_ref,
    tap_out,
    resp_out,
    grad_ref,
    ew,
    sw,
    taps,
    mixed,
    normed,
    spread,
    scaled,
    hid,
    act,
    energy,
    ratio,
    sums,
    back,
    back_hid,
    side_steps,
    tap_acc,
    resp_acc,
    inbox,
    stage,
    landed,
    local_sem,
    x_send,
    x_recv,
    y_send,
    y_recv,
    own_send,
    own_recv,
    f_send,
    f_recv,
    h_send,
    h_recv,
    p_send,
    p_recv,
    s_send,
    s_recv,
):
    micro, pix, channels = x_ref.shape
    units = sw.shape[0]
    e_rows, s_rows = expand_ref.shape[0], shrink_ref.shape[0]
    grp = lax.axis_index("groups")
    pos = lax.axis_index("pipe")
    me = lax.axis_index("dp")
    last = sections - 1
    high, low = me // 2, me % 2
    across = 2 * (1 - high) + low
    beside = 2 * high + (1 - low)
    other = 2 * (1 - high) + (1 - low)

    barrier = pltpu.get_barrier_semaphore()

    def greet(g, p, d):
        pl.semaphore_signal(barrier, inc=1, device_id=(g, p, d), device_id_type=MESH)

    greet(grp, pos, across)
    greet(grp, pos, beside)
    greet(grp, pos, other)
    greet(1 - grp, pos, me)

    @pl.when(pos > 0)
    def _():
        greet(grp, pos - 1, me)

    @pl.when(pos < last)
    def _():
        greet(grp, pos + 1, me)

    pl.semaphore_wait(
        barrier, 4 + jnp.where(pos > 0, 1, 0) + jnp.where(pos < last, 1, 0)
    )

    def piece(owner, half, c):
        if c < CHUNKS:
            size = e_rows // (2 * CHUNKS)
            start = owner * e_rows + half * (e_rows // 2) + c * size
            return ew.at[pl.ds(pl.multiple_of(start, 16), size), :]
        size = s_rows // (2 * CHUNKS)
        start = owner * s_rows + half * (s_rows // 2) + (c - CHUNKS) * size
        return sw.at[pl.ds(pl.multiple_of(start, 16), size), :]

    def own_piece(half, c):
        if c < CHUNKS:
            size = e_rows // (2 * CHUNKS)
            start = half * (e_rows // 2) + c * size
            return expand_ref.at[pl.ds(pl.multiple_of(start, 16), size), :]
        size = s_rows // (2 * CHUNKS)
        start = half * (s_rows // 2) + (c - CHUNKS) * size
        return shrink_ref.at[pl.ds(pl.multiple_of(start, 16), size), :]

    def remote(src, dst, send, recv, g, p, d):
        return pltpu.make_async_remote_copy(
            src_ref=src,
            dst_ref=dst,
            send_sem=send,
            recv_sem=recv,
            device_id=(g, p, d),
            device_id_type=MESH,
        )

    def x_copy(c, owner):
        return remote(
            own_piece(grp, c), piece(owner, grp, c), x_send.at[c], x_recv.at[c], grp, pos, across
        )

    def y_copy(c, half):
        spot = piece(across, half, c)
        return remote(spot, spot, y_send.at[c], y_recv.at[c], 1 - grp, pos, me)

    def f_copy(c, owner):
        spot = piece(owner, grp, c)
        return remote(spot, spot, f_send.at[c], f_recv.at[c], grp, pos, beside)

    def h_copy(c, owner):
        spot = piece(owner, 1 - grp, c)
        return remote(spot, spot, h_send.at[c], h_recv.at[c], grp, pos, beside)

    def shard(which, owner):
        if which == 0:
            return ew.at[pl.ds(pl.multiple_of(owner * e_rows, 16), e_rows), :]
        return sw.at[pl.ds(pl.multiple_of(owner * s_rows, 16), s_rows), :]

    def own_copy(which, owner):
        src = (expand_ref, shrink_ref)[which]
        return remote(
            src, shard(which, owner), own_send.at[which], own_recv.at[which], grp, pos, beside
        )

    for c in range(2 * CHUNKS):
        x_copy(c, me).start()
    for which in range(2):
        own_copy(which, me).start()
    locals_ = [
        pltpu.make_async_copy((expand_ref, shrink_ref)[w], shard(w, me), local_sem.at[w])
        for w in range(2)
    ]
    for copy in locals_:
        copy.start()

    def pass_x(c):
        x_copy(c, across).wait_recv()
        y_copy(c, grp).start()
        f_copy(c, across).start()

    def pass_y(c):
        y_copy(c, 1 - grp).wait_recv()
        h_copy(c, across).start()

    taps[...] = tap_ref[...].astype(jnp.float32)
    gain = gain_ref[...].astype(jnp.float32)

    def forward(slot):
        def tile(t, carry):
            lanes = pl.ds(pl.multiple_of(t * LANES, LANES), LANES)
            image = x_ref[plan_ref[0, slot], :, lanes].astype(jnp.float32).reshape(SIDE, SIDE, LANES)
            total = jnp.zeros_like(image)
            for col in range(KSIDE):
                moved = row_padded(shifted(image, col - MARGIN))
                for row in range(KSIDE):
                    tap = row * KSIDE + col
                    total = total + taps[tap : tap + 1, lanes][None] * moved[row : row + SIDE]
            mixed[:, lanes] = total.reshape(pix, LANES)
            return carry

        lax.fori_loop(0, channels // LANES, tile, 0)
        value = mixed[...]
        offset = value - jnp.mean(value, axis=-1, keepdims=True)
        scale = lax.rsqrt(jnp.mean(offset * offset, axis=-1, keepdims=True) + 1e-06)
        unit = offset * scale
        normed[slot] = unit
        spread[slot] = scale
        scaled[pl.ds(pl.multiple_of(slot * pix, pix), pix), :] = (unit * gain).astype(jnp.bfloat16)

    tap_acc[...] = jnp.zeros_like(tap_acc)
    resp_acc[...] = jnp.zeros_like(resp_acc)

    def passes(steps, count):
        for c in steps[:count]:
            pass_x(c)
            if c > 0:
                pass_y(c - 1)
        return steps[count:]

    first_part = list(range(CHUNKS + 1))
    for slot in range(micro):
        forward(slot)
        first_part = passes(first_part, 1)
    passes(first_part, CHUNKS)
    locals_[0].wait()
    own_copy(0, beside).wait_recv()
    for c in range(CHUNKS):
        f_copy(c, other).wait_recv()
        h_copy(c, other).wait_recv()

    def hidden_block(b, carry):
        cols = pl.ds(pl.multiple_of(b * F_BLOCK, F_BLOCK), F_BLOCK)
        result = jnp.dot(scaled[...], ew[:, cols], preferred_element_type=jnp.float32)
        hid[:, :, cols] = result.reshape(micro, pix, F_BLOCK)
        return carry

    lax.fori_loop(0, units // F_BLOCK, hidden_block, 0)
    second_part = passes(list(range(CHUNKS + 1, 2 * CHUNKS)), 1)

    resp_block = F_BLOCK

    def gelu(slot):
        def block(b, carry):
            cols = pl.ds(pl.multiple_of(b * resp_block, resp_block), resp_block)
            h = hid[slot, :, cols]
            erf_part = 0.5 * (1.0 + lax.erf(h * inverse_root_two))
            a = h * erf_part
            act[slot, :, cols] = a
            hid[slot, :, cols] = erf_part + h * jnp.exp(-0.5 * h * h) * inverse_root_tau
            energy[slot, :, cols] = jnp.sqrt(jnp.sum(a * a, axis=0, keepdims=True) + 1e-06)
            return carry

        lax.fori_loop(0, units // resp_block, block, 0)
        e = energy[slot]
        ratio[slot] = e / (jnp.mean(e, axis=-1, keepdims=True) + 1e-06)

    for slot in range(micro):
        gelu(slot)
        second_part = passes(second_part, 1)
    passes(second_part, CHUNKS)
    pass_y(2 * CHUNKS - 1)
    locals_[1].wait()
    own_copy(1, beside).wait_recv()
    for c in range(CHUNKS, 2 * CHUNKS):
        f_copy(c, other).wait_recv()
        h_copy(c, other).wait_recv()

    width = channels // PIECES

    def pipe_copy(slot, k, to):
        spot = (slot, slice(None), slice(k * width, (k + 1) * width))
        return remote(
            grad_ref.at[spot], inbox.at[spot], p_send.at[slot, k], p_recv.at[slot, k], grp, to, me
        )

    def backward(slot, carry):
        @pl.when(pos == last)
        def _():
            inbox[slot] = loss_ref[slot]

        @pl.when(pos < last)
        def _():
            for k in range(PIECES):
                pipe_copy(slot, k, pos + 1).wait_recv()

        up = inbox[slot]
        average = jnp.mean(energy[slot], axis=-1, keepdims=True) + 1e-06
        weight = jnp.zeros((1, 1), jnp.float32)
        for b in range(units // F_BLOCK):
            cols = slice(b * F_BLOCK, (b + 1) * F_BLOCK)
            br = lax.dot_general(up, sw[cols, :], NT, preferred_element_type=jnp.float32)
            back[:, cols] = br
            s = jnp.sum(br * act[slot, :, cols], axis=0, keepdims=True)
            resp_acc[:, cols] += s * ratio[slot, :, cols]
            w = s * resp_ref[:, cols].astype(jnp.float32)
            sums[:, cols] = w
            weight += jnp.sum(w * energy[slot, :, cols], axis=-1, keepdims=True)
        weight = weight / (average * average * units)
        inverse = 1.0 / average
        for b in range(units // F_BLOCK):
            cols = slice(b * F_BLOCK, (b + 1) * F_BLOCK)
            first = 1.0 + resp_ref[:, cols].astype(jnp.float32) * ratio[slot, :, cols]
            second = (sums[:, cols] * inverse - weight) / energy[slot, :, cols]
            ba = back[:, cols] * first + act[slot, :, cols] * second
            back_hid[:, cols] = (ba * hid[slot, :, cols]).astype(jnp.bfloat16)
        bs = jnp.zeros((pix, channels), jnp.float32)
        for b in range(units // F_BLOCK):
            cols = slice(b * F_BLOCK, (b + 1) * F_BLOCK)
            bs += lax.dot_general(
                back_hid[:, cols], ew[:, cols], NT, preferred_element_type=jnp.float32
            )
        q = bs * gain
        unit = normed[slot]
        mixed[...] = (
            q
            - jnp.mean(q, axis=-1, keepdims=True)
            - unit * jnp.mean(q * unit, axis=-1, keepdims=True)
        ) * spread[slot]

        def tile(t, inner):
            lanes = pl.ds(pl.multiple_of(t * LANES, LANES), LANES)
            image = mixed[:, lanes].reshape(SIDE, SIDE, LANES)
            total = inbox[slot, :, lanes].astype(jnp.float32).reshape(SIDE, SIDE, LANES)
            for col in range(KSIDE):
                plain = shifted(image, MARGIN - col)
                side_steps[col, :, lanes] = plain.reshape(pix, LANES)
                moved = row_padded(plain)
                for row in range(KSIDE):
                    tap = row * KSIDE + col
                    at = KSIDE - 1 - row
                    total = total + taps[tap : tap + 1, lanes][None] * moved[at : at + SIDE]
            grad_ref[slot, :, lanes] = total.reshape(pix, LANES).astype(jnp.bfloat16)
            return inner

        for k in range(PIECES):
            lax.fori_loop(k * width // LANES, (k + 1) * width // LANES, tile, 0)

            @pl.when(pos > 0)
            def _():
                pipe_copy(slot, k, pos - 1).start()

        def tap_tile(t, inner):
            lanes = pl.ds(pl.multiple_of(t * LANES, LANES), LANES)
            image = x_ref[plan_ref[0, slot], :, lanes].astype(jnp.float32).reshape(SIDE, SIDE, LANES)
            for col in range(KSIDE):
                moved = row_padded(side_steps[col, :, lanes].reshape(SIDE, SIDE, LANES))
                for row in range(KSIDE):
                    tap = row * KSIDE + col
                    at = KSIDE - 1 - row
                    tap_acc[tap, :, lanes] += jnp.sum(moved[at : at + SIDE] * image, axis=0)
            return inner

        lax.fori_loop(0, channels // LANES, tap_tile, 0)
        return carry

    lax.fori_loop(0, micro, backward, 0)

    totals = jnp.sum(tap_acc[...], axis=1)
    share = channels // 4
    pad = stage.shape[1] - TAPS - units // 4 // WINDOW
    for d in range(4):
        start = d * share // LANES * LANES
        rows = [totals[:, start : start + WINDOW]]
        for k in range(units // 4 // WINDOW):
            at = d * (units // 4) + k * WINDOW
            rows.append(resp_acc[:, at : at + WINDOW])
        rows.append(jnp.zeros((pad, WINDOW), jnp.float32))
        stage[d] = jnp.concatenate(rows, axis=0).astype(jnp.bfloat16)

    peers = (across, beside, other)

    def s_copy(k):
        return remote(stage.at[peers[k]], landed.at[k], s_send.at[k], s_recv.at[k], grp, pos, peers[k])

    for k in range(3):
        s_copy(k).start()
    for m in range(micro):
        slot = jnp.int32(0)
        for j in range(1, micro):
            slot = jnp.where(plan_ref[0, j] == m, j, slot)
        out_ref[m] = grad_ref[slot]
    total = stage[me].astype(jnp.float32)
    for k in range(3):
        s_copy(k).wait_recv()
        total = total + landed[k].astype(jnp.float32)
    edge = share - share // LANES * LANES
    odd = me * share % LANES != 0
    tap_out[...] = jnp.where(odd, total[:TAPS, edge : edge + share], total[:TAPS, :share])
    for k in range(units // 4 // WINDOW):
        resp_out[:, k * WINDOW : (k + 1) * WINDOW] = total[TAPS + k : TAPS + k + 1]

    for k in range(3):
        s_copy(k).wait_send()
    for c in range(2 * CHUNKS):
        x_copy(c, me).wait_send()
        y_copy(c, grp).wait_send()
        f_copy(c, across).wait_send()
        h_copy(c, across).wait_send()
    for which in range(2):
        own_copy(which, me).wait_send()

    @pl.when(pos > 0)
    def _():
        def drain(slot, carry):
            for k in range(PIECES):
                pipe_copy(slot, k, pos - 1).wait_send()
            return carry

        lax.fori_loop(0, micro, drain, 0)


def on_device(
    section_input,
    depth_kernel,
    norm_gain,
    expand_weight,
    shrink_weight,
    response_gain,
    loss_grad,
    plan,
):
    local_x = section_input[0]
    micro, pix, channels = local_x.shape
    units = expand_weight.shape[2]
    sections = lax.axis_size("pipe")
    share = channels // 4
    f32, bf16 = jnp.float32, jnp.bfloat16
    vmem = pl.BlockSpec(memory_space=pltpu.VMEM)
    smem = pl.BlockSpec(memory_space=pltpu.SMEM)
    anywhere = pl.BlockSpec(memory_space=pl.ANY)
    dma = pltpu.SemaphoreType.DMA
    grads, tap_share, resp_share = pl.pallas_call(
        functools.partial(kernel, sections),
        out_shape=(
            jax.ShapeDtypeStruct((micro, pix, channels), bf16),
            jax.ShapeDtypeStruct((TAPS, share), f32),
            jax.ShapeDtypeStruct((1, units // 4), f32),
        ),
        in_specs=[smem, vmem, vmem, vmem, anywhere, anywhere, vmem, vmem],
        out_specs=(vmem, vmem, vmem),
        scratch_shapes=[
            pltpu.VMEM((micro, pix, channels), bf16),
            pltpu.VMEM((channels, units), bf16),
            pltpu.VMEM((units, channels), bf16),
            pltpu.VMEM((TAPS, channels), f32),
            pltpu.VMEM((pix, channels), f32),
            pltpu.VMEM((micro, pix, channels), f32),
            pltpu.VMEM((micro, pix, 1), f32),
            pltpu.VMEM((micro * pix, channels), bf16),
            pltpu.VMEM((micro, pix, units), f32),
            pltpu.VMEM((micro, pix, units), f32),
            pltpu.VMEM((micro, 1, units), f32),
            pltpu.VMEM((micro, 1, units), f32),
            pltpu.VMEM((1, units), f32),
            pltpu.VMEM((pix, units), f32),
            pltpu.VMEM((pix, units), bf16),
            pltpu.VMEM((KSIDE, pix, channels), f32),
            pltpu.VMEM((TAPS, SIDE, channels), f32),
            pltpu.VMEM((1, units), f32),
            pltpu.VMEM((micro, pix, channels), bf16),
            pltpu.VMEM((4, 64, WINDOW), bf16),
            pltpu.VMEM((3, 64, WINDOW), bf16),
            dma((2,)),
            dma((2 * CHUNKS,)),
            dma((2 * CHUNKS,)),
            dma((2 * CHUNKS,)),
            dma((2 * CHUNKS,)),
            dma((2,)),
            dma((2,)),
            dma((2 * CHUNKS,)),
            dma((2 * CHUNKS,)),
            dma((2 * CHUNKS,)),
            dma((2 * CHUNKS,)),
            dma((micro, PIECES)),
            dma((micro, PIECES)),
            dma((3,)),
            dma((3,)),
        ],
        compiler_params=pltpu.CompilerParams(
            collective_id=0, has_side_effects=True, vmem_limit_bytes=52 * 1024 * 1024
        ),
    )(
        plan,
        local_x,
        depth_kernel[0],
        norm_gain,
        expand_weight[0],
        shrink_weight[0],
        response_gain,
        loss_grad,
    )
    return (grads[None], tap_share[None], resp_share)


def solution(mesh):
    if mesh.shape["dp"] != 4 or mesh.shape["groups"] != 2:
        raise ValueError("unsupported mesh")
    placed = (
        P("pipe", ("groups", "dp"), None, None),
        P("pipe", None, None),
        P("pipe", None),
        P("pipe", "dp", None),
        P("pipe", "dp", None),
        P("pipe", None),
        P(("groups", "dp"), None, None),
        P(("groups", "dp"), None),
    )
    return jax.shard_map(
        on_device,
        mesh=mesh,
        in_specs=placed,
        out_specs=(
            P("pipe", ("groups", "dp"), None, None),
            P(("groups", "pipe"), None, "dp"),
            P(("groups", "pipe"), "dp"),
        ),
        check_vma=False,
    )
```

```python
import functools

import jax
import jax.numpy as jnp
from jax import lax
from jax.experimental import pallas as pl
from jax.experimental.pallas import tpu as pltpu
from jax.sharding import PartitionSpec as P

KSIDE = 7
SIDE = 8
MARGIN = 3
TAPS = KSIDE * KSIDE
LANES = 128
WINDOW = 256
PIECES = 3

inverse_root_two = 0.7071067811865476
inverse_root_tau = 0.3989422804014327

MESH = pl.DeviceIdType.MESH
CHUNKS = 3
F_BLOCK = 512


def shifted(value, by):
    if by == 0:
        return value
    column = lax.broadcasted_iota(jnp.int32, value.shape, 1) + by
    moved = pltpu.roll(value, (-by) % SIDE, 1)
    return jnp.where((column >= 0) & (column < SIDE), moved, 0.0)


def row_padded(value):
    zeros = jnp.zeros((MARGIN,) + value.shape[1:], value.dtype)
    return jnp.concatenate([zeros, value, zeros], axis=0)


def kernel(
    sections,
    plan_ref,
    x_any,
    tap_any,
    gain_any,
    expand_ref,
    shrink_ref,
    resp_any,
    loss_any,
    out_ref,
    tap_out,
    resp_out,
    x_ref,
    tap_ref,
    gain_ref,
    resp_ref,
    loss_ref,
    grad_ref,
    ew,
    sw,
    ewt,
    swt,
    taps,
    mixed,
    normed,
    spread,
    scaled,
    hid,
    act,
    energy,
    ratio,
    sums,
    back,
    back_hid,
    side_steps,
    tap_acc,
    resp_acc,
    inbox,
    stage,
    landed,
    fetch_sem,
    local_sem,
    x_send,
    x_recv,
    y_send,
    y_recv,
    own_send,
    own_recv,
    f_send,
    f_recv,
    h_send,
    h_recv,
    p_send,
    p_recv,
    s_send,
    s_recv,
):
    micro, pix, channels = x_ref.shape
    units = sw.shape[0]
    e_rows, s_rows = expand_ref.shape[0], shrink_ref.shape[0]
    grp = lax.axis_index("groups")
    pos = lax.axis_index("pipe")
    me = lax.axis_index("dp")
    last = sections - 1
    high, low = me // 2, me % 2
    across = 2 * (1 - high) + low
    beside = 2 * high + (1 - low)
    other = 2 * (1 - high) + (1 - low)

    fetches = [
        pltpu.make_async_copy(src, dst, fetch_sem.at[k])
        for k, (src, dst) in enumerate(
            (
                (x_any, x_ref),
                (tap_any, tap_ref),
                (gain_any, gain_ref),
                (resp_any, resp_ref),
                (loss_any, loss_ref),
            )
        )
    ]
    for copy in fetches:
        copy.start()

    barrier = pltpu.get_barrier_semaphore()

    def greet(g, p, d):
        pl.semaphore_signal(barrier, inc=1, device_id=(g, p, d), device_id_type=MESH)

    greet(grp, pos, across)
    greet(grp, pos, beside)
    greet(grp, pos, other)
    greet(1 - grp, pos, me)

    @pl.when(pos > 0)
    def _():
        greet(grp, pos - 1, me)

    @pl.when(pos < last)
    def _():
        greet(grp, pos + 1, me)

    pl.semaphore_wait(
        barrier, 4 + jnp.where(pos > 0, 1, 0) + jnp.where(pos < last, 1, 0)
    )

    def piece(owner, half, c):
        if c < CHUNKS:
            size = e_rows // (2 * CHUNKS)
            start = owner * e_rows + half * (e_rows // 2) + c * size
            return ew.at[pl.ds(pl.multiple_of(start, 16), size), :]
        size = s_rows // (2 * CHUNKS)
        start = owner * s_rows + half * (s_rows // 2) + (c - CHUNKS) * size
        return sw.at[pl.ds(pl.multiple_of(start, 16), size), :]

    def own_piece(half, c):
        if c < CHUNKS:
            size = e_rows // (2 * CHUNKS)
            start = half * (e_rows // 2) + c * size
            return expand_ref.at[pl.ds(pl.multiple_of(start, 16), size), :]
        size = s_rows // (2 * CHUNKS)
        start = half * (s_rows // 2) + (c - CHUNKS) * size
        return shrink_ref.at[pl.ds(pl.multiple_of(start, 16), size), :]

    def remote(src, dst, send, recv, g, p, d):
        return pltpu.make_async_remote_copy(
            src_ref=src,
            dst_ref=dst,
            send_sem=send,
            recv_sem=recv,
            device_id=(g, p, d),
            device_id_type=MESH,
        )

    def x_copy(c, owner):
        return remote(
            own_piece(grp, c), piece(owner, grp, c), x_send.at[c], x_recv.at[c], grp, pos, across
        )

    def y_copy(c, half):
        spot = piece(across, half, c)
        return remote(spot, spot, y_send.at[c], y_recv.at[c], 1 - grp, pos, me)

    def f_copy(c, owner):
        spot = piece(owner, grp, c)
        return remote(spot, spot, f_send.at[c], f_recv.at[c], grp, pos, beside)

    def h_copy(c, owner):
        spot = piece(owner, 1 - grp, c)
        return remote(spot, spot, h_send.at[c], h_recv.at[c], grp, pos, beside)

    def shard(which, owner):
        if which == 0:
            return ew.at[pl.ds(pl.multiple_of(owner * e_rows, 16), e_rows), :]
        return sw.at[pl.ds(pl.multiple_of(owner * s_rows, 16), s_rows), :]

    def own_copy(which, owner):
        src = (expand_ref, shrink_ref)[which]
        return remote(
            src, shard(which, owner), own_send.at[which], own_recv.at[which], grp, pos, beside
        )

    for c in range(2 * CHUNKS):
        x_copy(c, me).start()
    for which in range(2):
        own_copy(which, me).start()
    locals_ = [
        pltpu.make_async_copy((expand_ref, shrink_ref)[w], shard(w, me), local_sem.at[w])
        for w in range(2)
    ]
    for copy in locals_:
        copy.start()

    def pass_x(c):
        x_copy(c, across).wait_recv()
        y_copy(c, grp).start()
        f_copy(c, across).start()

    def pass_y(c):
        y_copy(c, 1 - grp).wait_recv()
        h_copy(c, across).start()

    for copy in fetches:
        copy.wait()
    taps[...] = tap_ref[...].astype(jnp.float32)
    gain = gain_ref[...].astype(jnp.float32)

    def forward(slot):
        def tile(t, carry):
            lanes = pl.ds(pl.multiple_of(t * LANES, LANES), LANES)
            image = x_ref[plan_ref[0, slot], :, lanes].astype(jnp.float32).reshape(SIDE, SIDE, LANES)
            total = jnp.zeros_like(image)
            for col in range(KSIDE):
                moved = row_padded(shifted(image, col - MARGIN))
                for row in range(KSIDE):
                    tap = row * KSIDE + col
                    total = total + taps[tap : tap + 1, lanes][None] * moved[row : row + SIDE]
            mixed[:, lanes] = total.reshape(pix, LANES)
            return carry

        lax.fori_loop(0, channels // LANES, tile, 0)
        value = mixed[...]
        offset = value - jnp.mean(value, axis=-1, keepdims=True)
        scale = lax.rsqrt(jnp.mean(offset * offset, axis=-1, keepdims=True) + 1e-06)
        unit = offset * scale
        normed[slot] = unit
        spread[slot] = scale
        scaled[pl.ds(pl.multiple_of(slot * pix, pix), pix), :] = (unit * gain).astype(jnp.bfloat16)

    tap_acc[...] = jnp.zeros_like(tap_acc)
    resp_acc[...] = jnp.zeros_like(resp_acc)

    def passes(steps, count):
        for c in steps[:count]:
            pass_x(c)
            if c > 0:
                pass_y(c - 1)
        return steps[count:]

    first_part = list(range(CHUNKS + 1))
    for slot in range(micro):
        forward(slot)
        first_part = passes(first_part, 1)
    passes(first_part, CHUNKS)
    locals_[0].wait()
    own_copy(0, beside).wait_recv()
    for c in range(CHUNKS):
        f_copy(c, other).wait_recv()
        h_copy(c, other).wait_recv()

    def hidden_block(b, carry):
        cols = pl.ds(pl.multiple_of(b * F_BLOCK, F_BLOCK), F_BLOCK)
        result = jnp.dot(scaled[...], ew[:, cols], preferred_element_type=jnp.float32)
        hid[:, :, cols] = result.reshape(micro, pix, F_BLOCK)
        ewt[cols, :] = ew[:, cols].T
        return carry

    lax.fori_loop(0, units // F_BLOCK, hidden_block, 0)
    second_part = passes(list(range(CHUNKS + 1, 2 * CHUNKS)), 1)

    resp_block = F_BLOCK

    def gelu(slot):
        def block(b, carry):
            cols = pl.ds(pl.multiple_of(b * resp_block, resp_block), resp_block)
            h = hid[slot, :, cols]
            erf_part = 0.5 * (1.0 + lax.erf(h * inverse_root_two))
            a = h * erf_part
            act[slot, :, cols] = a
            hid[slot, :, cols] = erf_part + h * jnp.exp(-0.5 * h * h) * inverse_root_tau
            energy[slot, :, cols] = jnp.sqrt(jnp.sum(a * a, axis=0, keepdims=True) + 1e-06)
            return carry

        lax.fori_loop(0, units // resp_block, block, 0)
        e = energy[slot]
        ratio[slot] = e / (jnp.mean(e, axis=-1, keepdims=True) + 1e-06)

    for slot in range(micro):
        gelu(slot)
        second_part = passes(second_part, 1)
    passes(second_part, CHUNKS)
    def turn(owner):
        def block(b, carry):
            rows = pl.ds(pl.multiple_of(owner * s_rows + b * WINDOW, WINDOW), WINDOW)
            swt[:, rows] = sw[rows, :].T
            return carry

        lax.fori_loop(0, s_rows // WINDOW, block, 0)

    locals_[1].wait()
    turn(me)
    own_copy(1, beside).wait_recv()
    turn(beside)
    pass_y(2 * CHUNKS - 1)
    turn(across)
    for c in range(CHUNKS, 2 * CHUNKS):
        f_copy(c, other).wait_recv()
        h_copy(c, other).wait_recv()
    turn(other)

    width = channels // PIECES

    def pipe_copy(slot, k, to):
        spot = (slot, slice(None), slice(k * width, (k + 1) * width))
        return remote(
            grad_ref.at[spot], inbox.at[spot], p_send.at[slot, k], p_recv.at[slot, k], grp, to, me
        )

    def backward(slot, carry):
        @pl.when(pos == last)
        def _():
            inbox[slot] = loss_ref[slot]

        @pl.when(pos < last)
        def _():
            for k in range(PIECES):
                pipe_copy(slot, k, pos + 1).wait_recv()

        up = inbox[slot]
        average = jnp.mean(energy[slot], axis=-1, keepdims=True) + 1e-06
        weight = jnp.zeros((1, 1), jnp.float32)
        for b in range(units // F_BLOCK):
            cols = slice(b * F_BLOCK, (b + 1) * F_BLOCK)
            br = jnp.dot(up, swt[:, cols], preferred_element_type=jnp.float32)
            back[:, cols] = br
            s = jnp.sum(br * act[slot, :, cols], axis=0, keepdims=True)
            resp_acc[:, cols] += s * ratio[slot, :, cols]
            w = s * resp_ref[:, cols].astype(jnp.float32)
            sums[:, cols] = w
            weight += jnp.sum(w * energy[slot, :, cols], axis=-1, keepdims=True)
        weight = weight / (average * average * units)
        inverse = 1.0 / average
        for b in range(units // F_BLOCK):
            cols = slice(b * F_BLOCK, (b + 1) * F_BLOCK)
            first = 1.0 + resp_ref[:, cols].astype(jnp.float32) * ratio[slot, :, cols]
            second = (sums[:, cols] * inverse - weight) / energy[slot, :, cols]
            ba = back[:, cols] * first + act[slot, :, cols] * second
            back_hid[:, cols] = (ba * hid[slot, :, cols]).astype(jnp.bfloat16)
        bs = jnp.zeros((pix, channels), jnp.float32)
        for b in range(units // F_BLOCK):
            cols = slice(b * F_BLOCK, (b + 1) * F_BLOCK)
            bs += jnp.dot(back_hid[:, cols], ewt[cols, :], preferred_element_type=jnp.float32)
        q = bs * gain
        unit = normed[slot]
        mixed[...] = (
            q
            - jnp.mean(q, axis=-1, keepdims=True)
            - unit * jnp.mean(q * unit, axis=-1, keepdims=True)
        ) * spread[slot]

        def tile(t, inner):
            lanes = pl.ds(pl.multiple_of(t * LANES, LANES), LANES)
            image = mixed[:, lanes].reshape(SIDE, SIDE, LANES)
            total = inbox[slot, :, lanes].astype(jnp.float32).reshape(SIDE, SIDE, LANES)
            for col in range(KSIDE):
                plain = shifted(image, MARGIN - col)
                side_steps[col, :, lanes] = plain.reshape(pix, LANES)
                moved = row_padded(plain)
                for row in range(KSIDE):
                    tap = row * KSIDE + col
                    at = KSIDE - 1 - row
                    total = total + taps[tap : tap + 1, lanes][None] * moved[at : at + SIDE]
            grad_ref[slot, :, lanes] = total.reshape(pix, LANES).astype(jnp.bfloat16)
            return inner

        for k in range(PIECES):
            lax.fori_loop(k * width // LANES, (k + 1) * width // LANES, tile, 0)

            @pl.when(pos > 0)
            def _():
                pipe_copy(slot, k, pos - 1).start()

        def tap_tile(t, inner):
            lanes = pl.ds(pl.multiple_of(t * LANES, LANES), LANES)
            image = x_ref[plan_ref[0, slot], :, lanes].astype(jnp.float32).reshape(SIDE, SIDE, LANES)
            for col in range(KSIDE):
                moved = row_padded(side_steps[col, :, lanes].reshape(SIDE, SIDE, LANES))
                for row in range(KSIDE):
                    tap = row * KSIDE + col
                    at = KSIDE - 1 - row
                    tap_acc[tap, :, lanes] += jnp.sum(moved[at : at + SIDE] * image, axis=0)
            return inner

        lax.fori_loop(0, channels // LANES, tap_tile, 0)
        return carry

    lax.fori_loop(0, micro, backward, 0)

    totals = jnp.sum(tap_acc[...], axis=1)
    share = channels // 4
    pad = stage.shape[1] - TAPS - units // 4 // WINDOW
    for d in range(4):
        start = d * share // LANES * LANES
        rows = [totals[:, start : start + WINDOW]]
        for k in range(units // 4 // WINDOW):
            at = d * (units // 4) + k * WINDOW
            rows.append(resp_acc[:, at : at + WINDOW])
        rows.append(jnp.zeros((pad, WINDOW), jnp.float32))
        stage[d] = jnp.concatenate(rows, axis=0).astype(jnp.bfloat16)

    peers = (across, beside, other)

    def s_copy(k):
        return remote(stage.at[peers[k]], landed.at[k], s_send.at[k], s_recv.at[k], grp, pos, peers[k])

    for k in range(3):
        s_copy(k).start()
    for m in range(micro):
        slot = jnp.int32(0)
        for j in range(1, micro):
            slot = jnp.where(plan_ref[0, j] == m, j, slot)
        out_ref[m] = grad_ref[slot]
    total = stage[me].astype(jnp.float32)
    for k in range(3):
        s_copy(k).wait_recv()
        total = total + landed[k].astype(jnp.float32)
    edge = share - share // LANES * LANES
    odd = me * share % LANES != 0
    tap_out[...] = jnp.where(odd, total[:TAPS, edge : edge + share], total[:TAPS, :share])
    for k in range(units // 4 // WINDOW):
        resp_out[:, k * WINDOW : (k + 1) * WINDOW] = total[TAPS + k : TAPS + k + 1]

    for k in range(3):
        s_copy(k).wait_send()
    for c in range(2 * CHUNKS):
        x_copy(c, me).wait_send()
        y_copy(c, grp).wait_send()
        f_copy(c, across).wait_send()
        h_copy(c, across).wait_send()
    for which in range(2):
        own_copy(which, me).wait_send()

    @pl.when(pos > 0)
    def _():
        def drain(slot, carry):
            for k in range(PIECES):
                pipe_copy(slot, k, pos - 1).wait_send()
            return carry

        lax.fori_loop(0, micro, drain, 0)


def on_device(
    section_input,
    depth_kernel,
    norm_gain,
    expand_weight,
    shrink_weight,
    response_gain,
    loss_grad,
    plan,
):
    local_x = section_input[0]
    micro, pix, channels = local_x.shape
    units = expand_weight.shape[2]
    sections = lax.axis_size("pipe")
    share = channels // 4
    f32, bf16 = jnp.float32, jnp.bfloat16
    vmem = pl.BlockSpec(memory_space=pltpu.VMEM)
    smem = pl.BlockSpec(memory_space=pltpu.SMEM)
    anywhere = pl.BlockSpec(memory_space=pl.ANY)
    dma = pltpu.SemaphoreType.DMA
    grads, tap_share, resp_share = pl.pallas_call(
        functools.partial(kernel, sections),
        out_shape=(
            jax.ShapeDtypeStruct((micro, pix, channels), bf16),
            jax.ShapeDtypeStruct((TAPS, share), f32),
            jax.ShapeDtypeStruct((1, units // 4), f32),
        ),
        in_specs=[smem] + [anywhere] * 7,
        out_specs=(vmem, vmem, vmem),
        scratch_shapes=[
            pltpu.VMEM((micro, pix, channels), bf16),
            pltpu.VMEM((TAPS, channels), bf16),
            pltpu.VMEM((1, channels), bf16),
            pltpu.VMEM((1, units), bf16),
            pltpu.VMEM((micro, pix, channels), bf16),
            pltpu.VMEM((micro, pix, channels), bf16),
            pltpu.VMEM((channels, units), bf16),
            pltpu.VMEM((units, channels), bf16),
            pltpu.VMEM((units, channels), bf16),
            pltpu.VMEM((channels, units), bf16),
            pltpu.VMEM((TAPS, channels), f32),
            pltpu.VMEM((pix, channels), f32),
            pltpu.VMEM((micro, pix, channels), f32),
            pltpu.VMEM((micro, pix, 1), f32),
            pltpu.VMEM((micro * pix, channels), bf16),
            pltpu.VMEM((micro, pix, units), f32),
            pltpu.VMEM((micro, pix, units), f32),
            pltpu.VMEM((micro, 1, units), f32),
            pltpu.VMEM((micro, 1, units), f32),
            pltpu.VMEM((1, units), f32),
            pltpu.VMEM((pix, units), f32),
            pltpu.VMEM((pix, units), bf16),
            pltpu.VMEM((KSIDE, pix, channels), f32),
            pltpu.VMEM((TAPS, SIDE, channels), f32),
            pltpu.VMEM((1, units), f32),
            pltpu.VMEM((micro, pix, channels), bf16),
            pltpu.VMEM((4, 64, WINDOW), bf16),
            pltpu.VMEM((3, 64, WINDOW), bf16),
            dma((5,)),
            dma((2,)),
            dma((2 * CHUNKS,)),
            dma((2 * CHUNKS,)),
            dma((2 * CHUNKS,)),
            dma((2 * CHUNKS,)),
            dma((2,)),
            dma((2,)),
            dma((2 * CHUNKS,)),
            dma((2 * CHUNKS,)),
            dma((2 * CHUNKS,)),
            dma((2 * CHUNKS,)),
            dma((micro, PIECES)),
            dma((micro, PIECES)),
            dma((3,)),
            dma((3,)),
        ],
        compiler_params=pltpu.CompilerParams(
            collective_id=0, has_side_effects=True, vmem_limit_bytes=52 * 1024 * 1024
        ),
    )(
        plan,
        local_x,
        depth_kernel[0],
        norm_gain,
        expand_weight[0],
        shrink_weight[0],
        response_gain,
        loss_grad,
    )
    return (grads[None], tap_share[None], resp_share)


def solution(mesh):
    if mesh.shape["dp"] != 4 or mesh.shape["groups"] != 2:
        raise ValueError("unsupported mesh")
    placed = (
        P("pipe", ("groups", "dp"), None, None),
        P("pipe", None, None),
        P("pipe", None),
        P("pipe", "dp", None),
        P("pipe", "dp", None),
        P("pipe", None),
        P(("groups", "dp"), None, None),
        P(("groups", "dp"), None),
    )
    return jax.shard_map(
        on_device,
        mesh=mesh,
        in_specs=placed,
        out_specs=(
            P("pipe", ("groups", "dp"), None, None),
            P(("groups", "pipe"), None, "dp"),
            P(("groups", "pipe"), "dp"),
        ),
        check_vma=False,
    )
```

```python
import functools

import jax
import jax.numpy as jnp
from jax import lax
from jax.experimental import pallas as pl
from jax.experimental.pallas import tpu as pltpu
from jax.sharding import PartitionSpec as P

KSIDE = 7
SIDE = 8
MARGIN = 3
TAPS = KSIDE * KSIDE
LANES = 128
WINDOW = 256
PIECES = 3

inverse_root_two = 0.7071067811865476
inverse_root_tau = 0.3989422804014327

MESH = pl.DeviceIdType.MESH
CHUNKS = 3
F_BLOCK = 512


def shifted(value, by):
    if by == 0:
        return value
    column = lax.broadcasted_iota(jnp.int32, value.shape, 1) + by
    moved = pltpu.roll(value, (-by) % SIDE, 1)
    return jnp.where((column >= 0) & (column < SIDE), moved, 0.0)


def row_padded(value):
    zeros = jnp.zeros((MARGIN,) + value.shape[1:], value.dtype)
    return jnp.concatenate([zeros, value, zeros], axis=0)


def kernel(
    sections,
    plan_ref,
    x_any,
    tap_any,
    gain_any,
    expand_ref,
    shrink_ref,
    resp_any,
    loss_any,
    out_ref,
    tap_out,
    resp_out,
    x_ref,
    tap_ref,
    gain_ref,
    resp_ref,
    loss_ref,
    grad_ref,
    ew,
    sw,
    ewt,
    swt,
    taps,
    mixed,
    normed,
    spread,
    scaled,
    hid,
    act,
    energy,
    ratio,
    sums,
    back,
    back_hid,
    side_steps,
    tap_acc,
    resp_acc,
    inbox,
    stage,
    landed,
    fetch_sem,
    local_sem,
    x_send,
    x_recv,
    y_send,
    y_recv,
    own_send,
    own_recv,
    f_send,
    f_recv,
    h_send,
    h_recv,
    p_send,
    p_recv,
    s_send,
    s_recv,
):
    micro, pix, channels = x_ref.shape
    units = sw.shape[0]
    e_rows, s_rows = expand_ref.shape[0], shrink_ref.shape[0]
    grp = lax.axis_index("groups")
    pos = lax.axis_index("pipe")
    me = lax.axis_index("dp")
    last = sections - 1
    high, low = me // 2, me % 2
    across = 2 * (1 - high) + low
    beside = 2 * high + (1 - low)
    other = 2 * (1 - high) + (1 - low)

    fetches = [
        pltpu.make_async_copy(src, dst, fetch_sem.at[k])
        for k, (src, dst) in enumerate(
            (
                (x_any, x_ref),
                (tap_any, tap_ref),
                (gain_any, gain_ref),
                (resp_any, resp_ref),
                (loss_any, loss_ref),
            )
        )
    ]
    for copy in fetches:
        copy.start()

    barrier = pltpu.get_barrier_semaphore()

    def greet(g, p, d):
        pl.semaphore_signal(barrier, inc=1, device_id=(g, p, d), device_id_type=MESH)

    greet(grp, pos, across)
    greet(grp, pos, beside)
    greet(grp, pos, other)
    greet(1 - grp, pos, me)

    @pl.when(pos > 0)
    def _():
        greet(grp, pos - 1, me)

    @pl.when(pos < last)
    def _():
        greet(grp, pos + 1, me)

    pl.semaphore_wait(
        barrier, 4 + jnp.where(pos > 0, 1, 0) + jnp.where(pos < last, 1, 0)
    )

    def piece(owner, half, c):
        if c < CHUNKS:
            size = e_rows // (2 * CHUNKS)
            start = owner * e_rows + half * (e_rows // 2) + c * size
            return ew.at[pl.ds(pl.multiple_of(start, 16), size), :]
        size = s_rows // (2 * CHUNKS)
        start = owner * s_rows + half * (s_rows // 2) + (c - CHUNKS) * size
        return sw.at[pl.ds(pl.multiple_of(start, 16), size), :]

    def own_piece(half, c):
        if c < CHUNKS:
            size = e_rows // (2 * CHUNKS)
            start = half * (e_rows // 2) + c * size
            return expand_ref.at[pl.ds(pl.multiple_of(start, 16), size), :]
        size = s_rows // (2 * CHUNKS)
        start = half * (s_rows // 2) + (c - CHUNKS) * size
        return shrink_ref.at[pl.ds(pl.multiple_of(start, 16), size), :]

    def remote(src, dst, send, recv, g, p, d):
        return pltpu.make_async_remote_copy(
            src_ref=src,
            dst_ref=dst,
            send_sem=send,
            recv_sem=recv,
            device_id=(g, p, d),
            device_id_type=MESH,
        )

    def x_copy(c, owner):
        return remote(
            own_piece(grp, c), piece(owner, grp, c), x_send.at[c], x_recv.at[c], grp, pos, across
        )

    def y_copy(c, half):
        spot = piece(across, half, c)
        return remote(spot, spot, y_send.at[c], y_recv.at[c], 1 - grp, pos, me)

    def f_copy(c, owner):
        spot = piece(owner, grp, c)
        return remote(spot, spot, f_send.at[c], f_recv.at[c], grp, pos, beside)

    def h_copy(c, owner):
        spot = piece(owner, 1 - grp, c)
        return remote(spot, spot, h_send.at[c], h_recv.at[c], grp, pos, beside)

    def shard(which, owner):
        if which == 0:
            return ew.at[pl.ds(pl.multiple_of(owner * e_rows, 16), e_rows), :]
        return sw.at[pl.ds(pl.multiple_of(owner * s_rows, 16), s_rows), :]

    def own_copy(which, owner):
        src = (expand_ref, shrink_ref)[which]
        return remote(
            src, shard(which, owner), own_send.at[which], own_recv.at[which], grp, pos, beside
        )

    for c in range(2 * CHUNKS):
        x_copy(c, me).start()
    for which in range(2):
        own_copy(which, me).start()
    locals_ = [
        pltpu.make_async_copy((expand_ref, shrink_ref)[w], shard(w, me), local_sem.at[w])
        for w in range(2)
    ]
    for copy in locals_:
        copy.start()

    def pass_x(c):
        x_copy(c, across).wait_recv()
        y_copy(c, grp).start()
        f_copy(c, across).start()

    def pass_y(c):
        y_copy(c, 1 - grp).wait_recv()
        h_copy(c, across).start()

    for copy in fetches:
        copy.wait()
    taps[...] = tap_ref[...].astype(jnp.float32)
    gain = gain_ref[...].astype(jnp.float32)

    def forward(slot):
        def tile(t, carry):
            lanes = pl.ds(pl.multiple_of(t * LANES, LANES), LANES)
            image = x_ref[plan_ref[0, slot], :, lanes].astype(jnp.float32).reshape(SIDE, SIDE, LANES)
            total = jnp.zeros_like(image)
            for col in range(KSIDE):
                moved = row_padded(shifted(image, col - MARGIN))
                for row in range(KSIDE):
                    tap = row * KSIDE + col
                    total = total + taps[tap : tap + 1, lanes][None] * moved[row : row + SIDE]
            mixed[:, lanes] = total.reshape(pix, LANES)
            return carry

        lax.fori_loop(0, channels // LANES, tile, 0)
        value = mixed[...]
        offset = value - jnp.mean(value, axis=-1, keepdims=True)
        scale = lax.rsqrt(jnp.mean(offset * offset, axis=-1, keepdims=True) + 1e-06)
        unit = offset * scale
        normed[slot] = unit
        spread[slot] = scale
        scaled[pl.ds(pl.multiple_of(slot * pix, pix), pix), :] = (unit * gain).astype(jnp.bfloat16)

    tap_acc[...] = jnp.zeros_like(tap_acc)
    resp_acc[...] = jnp.zeros_like(resp_acc)

    def passes(steps, count):
        for c in steps[:count]:
            pass_x(c)
            if c > 0:
                pass_y(c - 1)
        return steps[count:]

    first_part = list(range(CHUNKS + 1))
    for slot in range(micro):
        forward(slot)
        first_part = passes(first_part, 1)
    passes(first_part, CHUNKS)
    locals_[0].wait()
    own_copy(0, beside).wait_recv()
    for c in range(CHUNKS):
        f_copy(c, other).wait_recv()
        h_copy(c, other).wait_recv()

    def hidden_block(b, carry):
        cols = pl.ds(pl.multiple_of(b * F_BLOCK, F_BLOCK), F_BLOCK)
        result = jnp.dot(scaled[...], ew[:, cols], preferred_element_type=jnp.float32)
        hid[:, :, cols] = result.reshape(micro, pix, F_BLOCK)
        ewt[cols, :] = ew[:, cols].T
        return carry

    lax.fori_loop(0, units // F_BLOCK, hidden_block, 0)
    second_part = passes(list(range(CHUNKS + 1, 2 * CHUNKS)), 1)

    resp_block = F_BLOCK

    def gelu(slot):
        def block(b, carry):
            cols = pl.ds(pl.multiple_of(b * resp_block, resp_block), resp_block)
            h = hid[slot, :, cols]
            erf_part = 0.5 * (1.0 + lax.erf(h * inverse_root_two))
            a = h * erf_part
            act[slot, :, cols] = a
            hid[slot, :, cols] = erf_part + h * jnp.exp(-0.5 * h * h) * inverse_root_tau
            energy[slot, :, cols] = jnp.sqrt(jnp.sum(a * a, axis=0, keepdims=True) + 1e-06)
            return carry

        lax.fori_loop(0, units // resp_block, block, 0)
        e = energy[slot]
        ratio[slot] = e / (jnp.mean(e, axis=-1, keepdims=True) + 1e-06)

    for slot in range(micro):
        gelu(slot)
        second_part = passes(second_part, 1)
    passes(second_part, CHUNKS)
    def turn(owner):
        def block(b, carry):
            rows = pl.ds(pl.multiple_of(owner * s_rows + b * WINDOW, WINDOW), WINDOW)
            swt[:, rows] = sw[rows, :].T
            return carry

        lax.fori_loop(0, s_rows // WINDOW, block, 0)

    locals_[1].wait()
    turn(me)
    own_copy(1, beside).wait_recv()
    turn(beside)
    pass_y(2 * CHUNKS - 1)
    turn(across)
    for c in range(CHUNKS, 2 * CHUNKS):
        f_copy(c, other).wait_recv()
        h_copy(c, other).wait_recv()
    turn(other)

    width = channels // PIECES

    def pipe_copy(slot, k, to):
        spot = (slot, slice(None), slice(k * width, (k + 1) * width))
        return remote(
            grad_ref.at[spot], inbox.at[spot], p_send.at[slot, k], p_recv.at[slot, k], grp, to, me
        )

    def backward(slot, carry):
        @pl.when(pos == last)
        def _():
            inbox[slot] = loss_ref[slot]

        @pl.when(pos < last)
        def _():
            for k in range(PIECES):
                pipe_copy(slot, k, pos + 1).wait_recv()

        up = inbox[slot]
        average = jnp.mean(energy[slot], axis=-1, keepdims=True) + 1e-06
        weight = jnp.zeros((1, 1), jnp.float32)
        for b in range(units // F_BLOCK):
            cols = slice(b * F_BLOCK, (b + 1) * F_BLOCK)
            br = jnp.dot(up, swt[:, cols], preferred_element_type=jnp.float32)
            back[:, cols] = br
            s = jnp.sum(br * act[slot, :, cols], axis=0, keepdims=True)
            resp_acc[:, cols] += s * ratio[slot, :, cols]
            w = s * resp_ref[:, cols].astype(jnp.float32)
            sums[:, cols] = w
            weight += jnp.sum(w * energy[slot, :, cols], axis=-1, keepdims=True)
        weight = weight / (average * average * units)
        inverse = 1.0 / average
        for b in range(units // F_BLOCK):
            cols = slice(b * F_BLOCK, (b + 1) * F_BLOCK)
            first = 1.0 + resp_ref[:, cols].astype(jnp.float32) * ratio[slot, :, cols]
            second = (sums[:, cols] * inverse - weight) / energy[slot, :, cols]
            ba = back[:, cols] * first + act[slot, :, cols] * second
            back_hid[:, cols] = (ba * hid[slot, :, cols]).astype(jnp.bfloat16)
        bs = jnp.zeros((pix, channels), jnp.float32)
        for b in range(units // F_BLOCK):
            cols = slice(b * F_BLOCK, (b + 1) * F_BLOCK)
            bs += jnp.dot(back_hid[:, cols], ewt[cols, :], preferred_element_type=jnp.float32)
        q = bs * gain
        unit = normed[slot]
        mixed[...] = (
            q
            - jnp.mean(q, axis=-1, keepdims=True)
            - unit * jnp.mean(q * unit, axis=-1, keepdims=True)
        ) * spread[slot]

        def tile(t, inner):
            lanes = pl.ds(pl.multiple_of(t * LANES, LANES), LANES)
            image = mixed[:, lanes].reshape(SIDE, SIDE, LANES)
            total = inbox[slot, :, lanes].astype(jnp.float32).reshape(SIDE, SIDE, LANES)
            for col in range(KSIDE):
                plain = shifted(image, MARGIN - col)
                side_steps[col, :, lanes] = plain.reshape(pix, LANES)
                moved = row_padded(plain)
                for row in range(KSIDE):
                    tap = row * KSIDE + col
                    at = KSIDE - 1 - row
                    total = total + taps[tap : tap + 1, lanes][None] * moved[at : at + SIDE]
            grad_ref[slot, :, lanes] = total.reshape(pix, LANES).astype(jnp.bfloat16)
            return inner

        for k in range(PIECES):
            lax.fori_loop(k * width // LANES, (k + 1) * width // LANES, tile, 0)

            @pl.when(pos > 0)
            def _():
                pipe_copy(slot, k, pos - 1).start()

        def tap_tile(t, inner):
            lanes = pl.ds(pl.multiple_of(t * LANES, LANES), LANES)
            image = x_ref[plan_ref[0, slot], :, lanes].astype(jnp.float32).reshape(SIDE, SIDE, LANES)
            for col in range(KSIDE):
                moved = row_padded(side_steps[col, :, lanes].reshape(SIDE, SIDE, LANES))
                for row in range(KSIDE):
                    tap = row * KSIDE + col
                    at = KSIDE - 1 - row
                    tap_acc[tap, :, lanes] += jnp.sum(moved[at : at + SIDE] * image, axis=0)
            return inner

        lax.fori_loop(0, channels // LANES, tap_tile, 0)
        return carry

    lax.fori_loop(0, micro, backward, 0)

    totals = jnp.sum(tap_acc[...], axis=1)
    share = channels // 4
    pad = stage.shape[1] - TAPS - units // 4 // WINDOW
    for d in range(4):
        start = d * share // LANES * LANES
        rows = [totals[:, start : start + WINDOW]]
        for k in range(units // 4 // WINDOW):
            at = d * (units // 4) + k * WINDOW
            rows.append(resp_acc[:, at : at + WINDOW])
        rows.append(jnp.zeros((pad, WINDOW), jnp.float32))
        stage[d] = jnp.concatenate(rows, axis=0).astype(jnp.bfloat16)

    peers = (across, beside, other)

    def s_copy(k):
        return remote(stage.at[peers[k]], landed.at[k], s_send.at[k], s_recv.at[k], grp, pos, peers[k])

    for k in range(3):
        s_copy(k).start()
    for m in range(micro):
        slot = jnp.int32(0)
        for j in range(1, micro):
            slot = jnp.where(plan_ref[0, j] == m, j, slot)
        out_ref[m] = grad_ref[slot]
    total = stage[me].astype(jnp.float32)
    for k in range(3):
        s_copy(k).wait_recv()
        total = total + landed[k].astype(jnp.float32)
    edge = share - share // LANES * LANES
    odd = me * share % LANES != 0
    tap_out[...] = jnp.where(odd, total[:TAPS, edge : edge + share], total[:TAPS, :share])
    for k in range(units // 4 // WINDOW):
        resp_out[:, k * WINDOW : (k + 1) * WINDOW] = total[TAPS + k : TAPS + k + 1]

    for k in range(3):
        s_copy(k).wait_send()
    for c in range(2 * CHUNKS):
        x_copy(c, me).wait_send()
        y_copy(c, grp).wait_send()
        f_copy(c, across).wait_send()
        h_copy(c, across).wait_send()
    for which in range(2):
        own_copy(which, me).wait_send()

    @pl.when(pos > 0)
    def _():
        def drain(slot, carry):
            for k in range(PIECES):
                pipe_copy(slot, k, pos - 1).wait_send()
            return carry

        lax.fori_loop(0, micro, drain, 0)


def on_device(
    section_input,
    depth_kernel,
    norm_gain,
    expand_weight,
    shrink_weight,
    response_gain,
    loss_grad,
    plan,
):
    local_x = section_input[0]
    micro, pix, channels = local_x.shape
    units = expand_weight.shape[2]
    sections = lax.axis_size("pipe")
    share = channels // 4
    f32, bf16 = jnp.float32, jnp.bfloat16
    vmem = pl.BlockSpec(memory_space=pltpu.VMEM)
    smem = pl.BlockSpec(memory_space=pltpu.SMEM)
    anywhere = pl.BlockSpec(memory_space=pl.ANY)
    dma = pltpu.SemaphoreType.DMA
    grads, tap_share, resp_share = pl.pallas_call(
        functools.partial(kernel, sections),
        out_shape=(
            jax.ShapeDtypeStruct((micro, pix, channels), bf16),
            jax.ShapeDtypeStruct((TAPS, share), f32),
            jax.ShapeDtypeStruct((1, units // 4), f32),
        ),
        in_specs=[smem] + [anywhere] * 7,
        out_specs=(vmem, vmem, vmem),
        scratch_shapes=[
            pltpu.VMEM((micro, pix, channels), bf16),
            pltpu.VMEM((TAPS, channels), bf16),
            pltpu.VMEM((1, channels), bf16),
            pltpu.VMEM((1, units), bf16),
            pltpu.VMEM((micro, pix, channels), bf16),
            pltpu.VMEM((micro, pix, channels), bf16),
            pltpu.VMEM((channels, units), bf16),
            pltpu.VMEM((units, channels), bf16),
            pltpu.VMEM((units, channels), bf16),
            pltpu.VMEM((channels, units), bf16),
            pltpu.VMEM((TAPS, channels), f32),
            pltpu.VMEM((pix, channels), f32),
            pltpu.VMEM((micro, pix, channels), f32),
            pltpu.VMEM((micro, pix, 1), f32),
            pltpu.VMEM((micro * pix, channels), bf16),
            pltpu.VMEM((micro, pix, units), f32),
            pltpu.VMEM((micro, pix, units), f32),
            pltpu.VMEM((micro, 1, units), f32),
            pltpu.VMEM((micro, 1, units), f32),
            pltpu.VMEM((1, units), f32),
            pltpu.VMEM((pix, units), f32),
            pltpu.VMEM((pix, units), bf16),
            pltpu.VMEM((KSIDE, pix, channels), f32),
            pltpu.VMEM((TAPS, SIDE, channels), f32),
            pltpu.VMEM((1, units), f32),
            pltpu.VMEM((micro, pix, channels), bf16),
            pltpu.VMEM((4, 64, WINDOW), bf16),
            pltpu.VMEM((3, 64, WINDOW), bf16),
            dma((5,)),
            dma((2,)),
            dma((2 * CHUNKS,)),
            dma((2 * CHUNKS,)),
            dma((2 * CHUNKS,)),
            dma((2 * CHUNKS,)),
            dma((2,)),
            dma((2,)),
            dma((2 * CHUNKS,)),
            dma((2 * CHUNKS,)),
            dma((2 * CHUNKS,)),
            dma((2 * CHUNKS,)),
            dma((micro, PIECES)),
            dma((micro, PIECES)),
            dma((3,)),
            dma((3,)),
        ],
        compiler_params=pltpu.CompilerParams(
            collective_id=0, has_side_effects=True, vmem_limit_bytes=62 * 1024 * 1024
        ),
    )(
        plan,
        local_x,
        depth_kernel[0],
        norm_gain,
        expand_weight[0],
        shrink_weight[0],
        response_gain,
        loss_grad,
    )
    return (grads[None], tap_share[None], resp_share)


def solution(mesh):
    if mesh.shape["dp"] != 4 or mesh.shape["groups"] != 2:
        raise ValueError("unsupported mesh")
    placed = (
        P("pipe", ("groups", "dp"), None, None),
        P("pipe", None, None),
        P("pipe", None),
        P("pipe", "dp", None),
        P("pipe", "dp", None),
        P("pipe", None),
        P(("groups", "dp"), None, None),
        P(("groups", "dp"), None),
    )
    return jax.shard_map(
        on_device,
        mesh=mesh,
        in_specs=placed,
        out_specs=(
            P("pipe", ("groups", "dp"), None, None),
            P(("groups", "pipe"), None, "dp"),
            P(("groups", "pipe"), "dp"),
        ),
        check_vma=False,
    )
```
